32 devices in a mesh: parts: 2 (over x), local: 16 (over z, y, core).
Axes of the slice: x: 2, y: 2, z: 4, core: 2. Of those that a mesh axis runs over, the one named last changes fastest.
Arguments:
- rows_in: bfloat16 [512, 7168], P(('parts', 'local')), parts along dimension 0, may hold values from -6 to 6
- routes: int32 [512, 4], P(('parts', 'local')), parts along dimension 0, may hold values from 0 to 15, all different within a row; in each aligned block of 16 rows (0 to 15, 16 to 31, ...) at most 8 rows name the same one
- comb_num: int32 [512, 4], P(('parts', 'local')), parts along dimension 0, may hold values from 1 to 63
- w_gate: bfloat16 [7168, 16384], P(None, 'local'), may hold values from -0.0625 to 0.0625
- w_up: bfloat16 [7168, 16384], P(None, 'local'), may hold values from -0.0625 to 0.0625
- w_down: bfloat16 [16384, 7168], P('local'), may hold values from -0.1875 to 0.1875
Outputs:
- mixed: bfloat16 [512, 7168], P(('parts', 'local')), parts along dimension 0
The draws below stay inside these ranges and needn't reach their ends.
There are 2 independent parts, one for each index of `parts`. The reference program is written for one: setup_inputs(seed, part) draws one part's arguments, and reference() takes and returns one part's arrays. A program takes and returns all parts, laid end to end along the dimension named above; an argument that names none is the same for every part. Nothing has to cross between parts.
Inputs may be any that keep to these rules, and one draw needn't show every extreme that they name: `routes`: each row names 4 different experts; among the rows of one device no expert is named by more than 8 rows, a bound that some block reaches.
All inputs are finite; a program needn't handle non-finite values.
Results may differ from the reference program's by a relative error of at most 0.0059.
Values may be sent and summed in bfloat16 or wider, within the bound.
No kernel may reach another device: no remote copies, remote signals or barrier semaphores. Data moves between devices by JAX's collectives and lax.ppermute only.
A program may use at most 128 MiB of HBM per device.

```python
import math
import jax
import jax.numpy as jnp
import numpy as np
from jax import lax

D = 7168
HID = 1024
E = 16
TOP = 4
ROWS_DEV = 16
CAP = 8
SPLIT = 1
ROWS = 256
N_LOCAL = 16


def place_ends(drawn, key, least, high):
    longest = drawn.shape.index(max(drawn.shape))
    spots = []
    for shift in (0, 1):
        where = [jax.random.randint(jax.random.fold_in(key, axis), (), 0, length) for axis, length in enumerate(drawn.shape)]
        where[longest] = (where[longest] + shift) % drawn.shape[longest]
        spots.append(tuple(where))
    return drawn.at[spots[0]].set(least).at[spots[1]].set(high)


def levels(stream_key, dims, cuts, least, high):
    def one(dim, blocks):
        heights = jax.random.uniform(jax.random.fold_in(jax.random.fold_in(stream_key, 6), dim), (blocks,), jnp.float32, least / len(cuts), high / len(cuts))
        return jnp.repeat(jnp.exp(heights), dims[dim] // blocks).reshape((-1,) + (1,) * (len(dims) - dim - 1))

    level = one(*cuts[0])
    for cut in cuts[1:]:
        level = level * one(*cut)
    return level


def deal_out(key, own, number, rows, number_of, top, bound, skew):
    ranking = jax.random.permutation(key, number_of)
    crowded, usual = portions_of(number_of, rows * top, bound, skew, True), portions_of(number_of, rows * top, bound, skew, False)
    places = jnp.arange(number_of)

    def named(tallies, offset_by):
        used = int((tallies > 0).sum())
        fixed = max(1, used // 4)
        passed = fixed + (places - fixed + offset_by * (used - fixed)) % max(1, number_of - fixed)
        return jnp.zeros((number_of,), jnp.int32).at[ranking[jnp.where(places < fixed, places, passed)]].set(jnp.asarray(tallies, jnp.int32))

    tallies = jnp.where(number % 4 == 0, named(crowded, number // 4), named(usual, number - number // 4 - 1))
    mixed = jax.random.permutation(jax.random.fold_in(own, 3), number_of)
    donor, receiver = mixed[0:number_of // 2 * 2:2], mixed[1:number_of // 2 * 2:2]
    room = jnp.minimum(tallies[donor] - 1, bound - tallies[receiver]) // 2
    room = jnp.where((donor == ranking[0]) | (receiver == ranking[0]) | (tallies[receiver] == 0), 0, jnp.maximum(room, 0))
    passed = jax.random.randint(jax.random.fold_in(own, 4), (number_of // 2,), 0, 1 << 20) % (room + 1)
    tallies = tallies.at[donor].add(-passed).at[receiver].add(passed)
    items = jnp.searchsorted(jnp.cumsum(tallies), jnp.arange(rows * top), side="right").astype(jnp.int32)
    grid = items.reshape(top, rows).T
    grid = grid[jax.random.permutation(jax.random.fold_in(own, 1), rows)]
    offset_by = jax.random.randint(jax.random.fold_in(own, 2), (rows, 1), 0, top)
    return jnp.take_along_axis(grid, (jnp.arange(top)[None, :] + offset_by) % top, axis=1)


def portions_of(number_of, total, reach, lean, full):
    loads = [(1 << 20) // math.isqrt(grade ** lean) + 1 for grade in range(1, number_of + 1)]
    largest = reach if full else min(reach, max(-(-total // number_of), total * loads[0] // sum(loads)))
    least = 1 if total - largest >= number_of - 1 else 0
    given, surplus = [largest] + [least] * (number_of - 1), total - largest - least * (number_of - 1)
    while surplus > 0:
        candidates = [i for i in range(1, number_of) if given[i] < largest] or [i for i in range(1, number_of) if given[i] < reach]
        whole, left = sum([loads[i] for i in candidates]), surplus
        for i in candidates:
            addition = min(reach - given[i], max(1, left * loads[i] // whole), surplus)
            given[i] = given[i] + addition
            surplus = surplus - addition
    return np.array(given)


def normal_values(stream_key, shape, scale, reach, cuts=(), kind=jnp.bfloat16):
    drawn = jax.random.normal(stream_key, shape, jnp.float32) * scale
    if len(cuts) > 0:
        drawn = levels(stream_key, shape, cuts, -0.22, 0.18) * drawn
    return jnp.clip(drawn, min=-reach, max=reach).astype(kind)


def setup_inputs(seed: int = 0, part: int = 0) -> dict:
    seeds = jax.random.split(jax.random.key(seed), 7)
    part_splits = jax.random.split(jax.random.fold_in(seeds[6], part), 7)
    rows_in = normal_values(part_splits[0], (ROWS, D), 1.0, 6.0, ((0, 16),))
    routes_keys = jax.random.split(jax.random.fold_in(part_splits[1], 1), ROWS // ROWS_DEV)
    routes_turns = jax.random.permutation(jax.random.fold_in(part_splits[1], 3), ROWS // ROWS_DEV)
    routes = jax.vmap(lambda own, number: deal_out(jax.random.fold_in(part_splits[1], 2), own, number, ROWS_DEV, E, TOP, CAP, 2))(routes_keys, routes_turns).reshape((ROWS, TOP))
    comb_num = place_ends(jax.random.randint(part_splits[2], (ROWS, TOP), 1, 64), jax.random.fold_in(part_splits[2], 1), 1, 63).astype(jnp.int32)
    w_gate = normal_values(seeds[3], (D, E * HID), D ** -0.5, 0.0625, ((1, 16),))
    w_up = normal_values(seeds[4], (D, E * HID), D ** -0.5, 0.0625, ((1, 16),))
    w_down = normal_values(seeds[5], (E * HID, D), HID ** -0.5, 0.1875, ((0, 16),))
    return dict(rows_in=rows_in, routes=routes, comb_num=comb_num, w_gate=w_gate, w_up=w_up, w_down=w_down)


denominator = 64.0


def expert_apply(items, gate_cols, up_cols, down_rows):
    gate_pre = jnp.dot(items, gate_cols, preferred_element_type=jnp.float32)
    up_pre = jnp.dot(items, up_cols, preferred_element_type=jnp.float32)
    hidden = (jax.nn.silu(gate_pre) * up_pre).astype(jnp.bfloat16)
    block_size = HID // SPLIT
    total = jnp.zeros((items.shape[0], D), jnp.float32)
    for quarter in range(SPLIT):
        piece = jnp.dot(hidden[:, quarter * block_size:(quarter + 1) * block_size],
                        down_rows[quarter * block_size:(quarter + 1) * block_size],
                        preferred_element_type=jnp.float32).astype(jnp.bfloat16)
        total = total + lax.optimization_barrier(piece).astype(jnp.float32)
    return total


def reference(rows_in, routes, comb_num, w_gate, w_up, w_down):
    total_rows = rows_in.shape[0]
    flat_ids = routes.reshape(-1).astype(jnp.int32)
    assigned = total_rows * TOP
    capacity = N_LOCAL * CAP
    row_of = (jnp.arange(assigned, dtype=jnp.int32) // TOP).astype(jnp.int32)

    def one_expert(expert, collected):
        expert = jnp.asarray(expert).astype(jnp.int32)
        chosen = flat_ids == expert
        slot_rank = (jnp.cumsum(chosen.astype(jnp.int32)) - 1).astype(jnp.int32)
        position = jnp.where(chosen, slot_rank, capacity).astype(jnp.int32)
        row_index = jnp.zeros((capacity + 1,), jnp.int32).at[position].set(row_of)[:capacity]
        items = rows_in[row_index]
        start = (expert * HID).astype(jnp.int32)
        gate_cols = lax.dynamic_slice_in_dim(w_gate, start, HID, 1)
        up_cols = lax.dynamic_slice_in_dim(w_up, start, HID, 1)
        down_rows = lax.dynamic_slice_in_dim(w_down, start, HID, 0)
        result = expert_apply(items, gate_cols, up_cols, down_rows)
        gathered = result[jnp.clip(slot_rank, 0, capacity - 1)]
        return jnp.where(chosen[:, None], gathered, collected)

    collected = lax.fori_loop(0, E, one_expert, jnp.zeros((assigned, D), jnp.float32))
    weights = comb_num.astype(jnp.float32) / denominator
    mixed = jnp.sum(collected.reshape(total_rows, TOP, D) * weights[:, :, None], axis=1)
    return mixed.astype(jnp.bfloat16)
```

```python
import functools

import jax
import jax.numpy as jnp
from jax import lax
from jax.experimental import pallas as pl
from jax.experimental.pallas import tpu as pltpu
from jax.sharding import PartitionSpec as P

E = 16
CAP = 8
LANES = 128
AHEAD = 5
denominator = 64.0
VMEM = pl.BlockSpec(memory_space=pltpu.VMEM)
SMEM = pl.BlockSpec(memory_space=pltpu.SMEM)
ANY = pl.BlockSpec(memory_space=pl.ANY)
HBM = pl.BlockSpec(memory_space=pltpu.HBM)


def exchange(x, distance):
    n = lax.axis_size("local")
    return lax.ppermute(x, "local", [(i, i ^ distance) for i in range(n)])


def pack_kernel(rows_ref, routes_ref, comb_ref, out_ref):
    rows, width = rows_ref.shape
    out_ref[:, :width] = rows_ref[...]
    sub = lax.broadcasted_iota(jnp.int32, (LANES, rows), 0)
    table = jnp.zeros((LANES, rows), jnp.int32)
    for k in range(routes_ref.shape[0]):
        table = jnp.where(sub == routes_ref[k : k + 1, :], comb_ref[k : k + 1, :], table)
    same = lax.broadcasted_iota(jnp.int32, (rows, rows), 0) == lax.broadcasted_iota(jnp.int32, (rows, rows), 1)
    turned = lax.dot_general(
        same.astype(jnp.float32).astype(jnp.bfloat16),
        table.astype(jnp.float32).astype(jnp.bfloat16),
        (((1,), (1,)), ((), ())), preferred_element_type=jnp.float32,
    )
    out_ref[:, width:] = turned.astype(jnp.bfloat16)


def pack(rows, routes, comb):
    return pl.pallas_call(
        pack_kernel,
        out_shape=jax.ShapeDtypeStruct((rows.shape[0], rows.shape[1] + LANES), rows.dtype),
        in_specs=[VMEM] * 3,
        out_specs=VMEM,
        name="pack",
    )(rows, routes.T, comb.T)


def tile_of(width, most):
    return max(t for t in range(LANES, most + 1, LANES) if width % t == 0)


def advance(copies, i):
    copies[i].wait()
    if i + AHEAD < len(copies):
        copies[i + AHEAD].start()


def expert_kernel(blocks, expert_ref, *refs):
    block_refs, refs = refs[:blocks], refs[blocks:]
    gate_hbm, up_hbm, down_hbm, refs = refs[0], refs[1], refs[2], refs[3:]
    keep_out, send_out, hidden_ref, combine_ref, refs = *refs[:4], refs[4:]
    rows_ref, gate_ref, up_ref, down_ref, gate_sum, up_sum, sems, weight_sems = refs
    count, total = rows_ref.shape
    width = total - LANES
    block = count // blocks
    slots = hidden_ref.shape[0]
    deep = tile_of(width, 1024)
    steps = width // deep

    copies = [
        pltpu.make_async_copy(ref, rows_ref.at[pl.ds(i * block, block), :], sems.at[i])
        for i, ref in enumerate(block_refs)
    ]
    near = []
    for j in range(steps):
        c = pl.ds(j * deep, deep)
        near.append(pltpu.make_async_copy(gate_hbm.at[c, :], gate_ref.at[c, :], weight_sems.at[2 * j]))
        near.append(pltpu.make_async_copy(up_hbm.at[c, :], up_ref.at[c, :], weight_sems.at[2 * j + 1]))
    for j in range(steps):
        c = pl.ds(j * deep, deep)
        near.append(
            pltpu.make_async_copy(down_hbm.at[:, c], down_ref.at[:, c], weight_sems.at[2 * steps + j])
        )
    for copy in copies + near[:AHEAD]:
        copy.start()
    for copy in copies:
        copy.wait()

    table = rows_ref[:, width:]
    mine = (lax.broadcasted_iota(jnp.int32, (8, LANES), 1) == expert_ref[0]).astype(jnp.float32)
    along = lax.dot_general(
        mine.astype(jnp.bfloat16), table, (((1,), (1,)), ((), ())),
        preferred_element_type=jnp.float32,
    )
    down_col = jnp.sum(table.astype(jnp.float32) * mine[:1, :], axis=1, keepdims=True)
    r = lax.broadcasted_iota(jnp.int32, (count, count), 0)
    s = lax.broadcasted_iota(jnp.int32, (count, count), 1)
    same = (r // block) == (s // block)
    before = (same & (r < s)).astype(jnp.float32).astype(jnp.bfloat16)
    after = (same & (s < r)).astype(jnp.float32).astype(jnp.bfloat16)
    chosen = (along > 0).astype(jnp.float32)
    rank = jnp.dot(chosen.astype(jnp.bfloat16), before, preferred_element_type=jnp.float32)
    start = (lax.broadcasted_iota(jnp.int32, (8, count), 1) // block) * CAP
    slot = jnp.where(along > 0, rank.astype(jnp.int32) + start, slots)[:1, :]
    place = (lax.broadcasted_iota(jnp.int32, (slots, count), 0) == slot)
    place = place.astype(jnp.float32).astype(jnp.bfloat16)
    chosen_col = jnp.broadcast_to((down_col > 0).astype(jnp.float32), (count, LANES))
    rank_col = jnp.dot(after, chosen_col.astype(jnp.bfloat16), preferred_element_type=jnp.float32)
    start_col = (lax.broadcasted_iota(jnp.int32, (count, 1), 0) // block) * CAP
    slot_col = rank_col[:, :1].astype(jnp.int32) + start_col
    combine = jnp.where(
        lax.broadcasted_iota(jnp.int32, (count, slots), 1) == slot_col,
        down_col / denominator, 0.0,
    ).astype(jnp.bfloat16)

    combine_ref[...] = combine

    for j in range(steps):
        c = pl.ds(j * deep, deep)
        items = jnp.dot(place, rows_ref[:, c], preferred_element_type=jnp.float32)
        items = items.astype(jnp.bfloat16)
        advance(near, 2 * j)
        gate = jnp.dot(items, gate_ref[c, :], preferred_element_type=jnp.float32)
        advance(near, 2 * j + 1)
        up = jnp.dot(items, up_ref[c, :], preferred_element_type=jnp.float32)
        if j > 0:
            gate, up = gate_sum[...] + gate, up_sum[...] + up
        gate_sum[...], up_sum[...] = gate, up
    gate = gate_sum[...]
    hidden_ref[...] = (gate / (1.0 + jnp.exp(-gate)) * up_sum[...]).astype(jnp.bfloat16)

    spread(
        hidden_ref, combine_ref, 0, down_ref, near, 2 * steps, deep, (keep_out, send_out)
    )


def spread(hidden_ref, combine_ref, first, down_ref, copies, passed, deep, outs):
    count = sum(out.shape[0] for out in outs)
    for j in range(len(copies) - passed):
        advance(copies, passed + j)
        c = pl.ds(j * deep, deep)
        piece = jnp.dot(
            hidden_ref[...], down_ref[:, c], preferred_element_type=jnp.float32
        ).astype(jnp.bfloat16)
        part = jnp.dot(
            combine_ref[first : first + count, :], piece, preferred_element_type=jnp.float32
        ).astype(jnp.bfloat16)
        start = 0
        for out in outs:
            out[:, c] = part[start : start + out.shape[0], :]
            start += out.shape[0]


def rest_kernel(first, hidden_ref, combine_ref, down_hbm, after_ref, *refs):
    outs, down_ref, sems = refs[:-2], refs[-2], refs[-1]
    steps = sems.shape[0]
    deep = down_ref.shape[1] // steps
    copies = [
        pltpu.make_async_copy(
            down_hbm.at[:, pl.ds(j * deep, deep)], down_ref.at[:, pl.ds(j * deep, deep)], sems.at[j]
        )
        for j in range(steps)
    ]
    for copy in copies[:AHEAD]:
        copy.start()
    spread(hidden_ref, combine_ref, first, down_ref, copies, 0, deep, outs)


def expert_rest(hidden, combine, w_down, after, first, pieces):
    width = w_down.shape[1]
    return pl.pallas_call(
        functools.partial(rest_kernel, first),
        out_shape=[jax.ShapeDtypeStruct((rows, width), jnp.bfloat16) for rows in pieces],
        in_specs=[VMEM, VMEM, HBM, ANY],
        out_specs=[VMEM] * len(pieces),
        scratch_shapes=[
            pltpu.VMEM(w_down.shape, jnp.bfloat16),
            pltpu.SemaphoreType.DMA((width // tile_of(width, 1024),)),
        ],
        compiler_params=pltpu.CompilerParams(vmem_limit_bytes=48 << 20),
        cost_estimate=pl.CostEstimate(
            flops=4 * hidden.shape[0] * w_down.size, bytes_accessed=w_down.size * 2, transcendentals=0
        ),
        name="rest",
    )(hidden, combine, pltpu.with_memory_space_constraint(w_down, pltpu.HBM), after)


def expert_part(expert, blocks, w_gate, w_up, w_down, piece):
    n = len(blocks)
    block, total = blocks[0].shape
    width = total - LANES
    units = w_gate.shape[1]
    count = n * block
    slots = n * CAP
    flops = 2 * slots * units * width * 3
    weights = [pltpu.with_memory_space_constraint(w, pltpu.HBM) for w in (w_gate, w_up, w_down)]
    return pl.pallas_call(
        functools.partial(expert_kernel, n),
        out_shape=[
            jax.ShapeDtypeStruct((piece, width), jnp.bfloat16),
            jax.ShapeDtypeStruct((piece, width), jnp.bfloat16),
            jax.ShapeDtypeStruct((slots, units), jnp.bfloat16),
            jax.ShapeDtypeStruct((count, slots), jnp.bfloat16),
        ],
        in_specs=[SMEM] + [ANY] * n + [HBM] * 3,
        out_specs=[VMEM] * 4,
        scratch_shapes=[
            pltpu.VMEM((count, total), jnp.bfloat16),
            pltpu.VMEM(w_gate.shape, jnp.bfloat16),
            pltpu.VMEM(w_up.shape, jnp.bfloat16),
            pltpu.VMEM(w_down.shape, jnp.bfloat16),
            pltpu.VMEM((slots, units), jnp.float32),
            pltpu.VMEM((slots, units), jnp.float32),
            pltpu.SemaphoreType.DMA((n,)),
            pltpu.SemaphoreType.DMA((3 * width // tile_of(width, 1024),)),
        ],
        compiler_params=pltpu.CompilerParams(vmem_limit_bytes=58 << 20),
        cost_estimate=pl.CostEstimate(
            flops=flops, bytes_accessed=w_down.size * 6, transcendentals=0
        ),
        name="expert",
    )(expert, *blocks, *weights)


def add(a, b, after=None):
    total = a.astype(jnp.float32) + b.astype(jnp.float32)
    if after is not None:
        total = total + after[0, 0].astype(jnp.float32) * 0.0
    return total.astype(jnp.bfloat16)


def on_device(rows_in, routes, comb_num, w_gate, w_up, w_down):
    n = lax.axis_size("local")
    me = lax.axis_index("local")
    b = rows_in.shape[0]
    expert = (me // (n // E)).astype(jnp.int32).reshape(1)
    far = range(n - 4, 4, -4)

    own = pack(rows_in, routes, comb_num)
    got = {0: own}
    got[n - 4] = exchange(own, n - 4)
    got[2] = exchange(own, 2)
    got[4] = exchange(own, 4)
    got[1] = exchange(own, 1)
    got[6] = exchange(got[2], 4)
    for k in far[1:]:
        got[k] = exchange(own, k)
    for k in far:
        got[k | 2] = exchange(got[k], 2)
    for k in range(2, n, 2):
        got[k | 1] = exchange(got[k], 1)

    first = n - 4
    planes = [*far, 4, 0]
    order = [k | i for k in planes for i in (0, 2, 1, 3)]
    keep, send, hidden, combine = expert_part(
        expert, [got[k] for k in order], w_gate, w_up, w_down, 2 * b
    )
    both = {first: add(keep, exchange(send, 1))}
    parts = expert_rest(hidden, combine, w_down, both[first], 4 * b, (2 * b,) * (n // 2 - 2))
    last = both[first]
    for i, k in enumerate(planes[1:]):
        last = both[k] = add(parts[2 * i], exchange(parts[2 * i + 1], 1), last)
    last = None
    came = []
    for k in planes:
        last = add(both[k][:b], exchange(both[k][b:], 2), last)
        came.append(exchange(last, k) if k else last)
    total = came[0].astype(jnp.float32)
    for piece in came[1:]:
        total = total + piece.astype(jnp.float32)
    return total.astype(jnp.bfloat16)


def solution(mesh):
    in_specs = (
        P(("parts", "local"), None),
        P(("parts", "local"), None),
        P(("parts", "local"), None),
        P(None, "local"),
        P(None, "local"),
        P("local", None),
    )
    out_specs = P(("parts", "local"), None)
    return jax.shard_map(
        on_device, mesh=mesh, in_specs=in_specs, out_specs=out_specs, check_vma=False
    )
```

```python
import functools

import jax
import jax.numpy as jnp
from jax import lax
from jax.experimental import pallas as pl
from jax.experimental.pallas import tpu as pltpu
from jax.sharding import PartitionSpec as P

E = 16
CAP = 8
LANES = 128
RING = 7
EARLY = 6
denominator = 64.0
VMEM = pl.BlockSpec(memory_space=pltpu.VMEM)
SMEM = pl.BlockSpec(memory_space=pltpu.SMEM)
ANY = pl.BlockSpec(memory_space=pl.ANY)
HBM = pl.BlockSpec(memory_space=pltpu.HBM)


def exchange(x, distance):
    n = lax.axis_size("local")
    return lax.ppermute(x, "local", [(i, i ^ distance) for i in range(n)])


def pack_kernel(rows_ref, routes_ref, comb_ref, out_ref):
    rows, width = rows_ref.shape
    out_ref[:, :width] = rows_ref[...]
    sub = lax.broadcasted_iota(jnp.int32, (LANES, rows), 0)
    table = jnp.zeros((LANES, rows), jnp.int32)
    for k in range(routes_ref.shape[0]):
        table = jnp.where(sub == routes_ref[k : k + 1, :], comb_ref[k : k + 1, :], table)
    same = lax.broadcasted_iota(jnp.int32, (rows, rows), 0) == lax.broadcasted_iota(jnp.int32, (rows, rows), 1)
    turned = lax.dot_general(
        same.astype(jnp.float32).astype(jnp.bfloat16),
        table.astype(jnp.float32).astype(jnp.bfloat16),
        (((1,), (1,)), ((), ())), preferred_element_type=jnp.float32,
    )
    out_ref[:, width:] = turned.astype(jnp.bfloat16)


def pack(rows, routes, comb):
    return pl.pallas_call(
        pack_kernel,
        out_shape=jax.ShapeDtypeStruct((rows.shape[0], rows.shape[1] + LANES), rows.dtype),
        in_specs=[VMEM] * 3,
        out_specs=VMEM,
        name="pack",
    )(rows, routes.T, comb.T)


def routing(table, expert, block):
    count = table.shape[0]
    slots = count // block * CAP
    mine = (lax.broadcasted_iota(jnp.int32, (8, LANES), 1) == expert).astype(jnp.float32)
    along = lax.dot_general(
        mine.astype(jnp.bfloat16), table, (((1,), (1,)), ((), ())),
        preferred_element_type=jnp.float32,
    )
    down = jnp.sum(table.astype(jnp.float32) * mine[:1, :], axis=1, keepdims=True)
    r = lax.broadcasted_iota(jnp.int32, (count, count), 0)
    s = lax.broadcasted_iota(jnp.int32, (count, count), 1)
    same = (r // block) == (s // block)
    before = (same & (r < s)).astype(jnp.float32).astype(jnp.bfloat16)
    after = (same & (s < r)).astype(jnp.float32).astype(jnp.bfloat16)
    chosen = (along > 0).astype(jnp.float32)
    rank = jnp.dot(chosen.astype(jnp.bfloat16), before, preferred_element_type=jnp.float32)
    start = (lax.broadcasted_iota(jnp.int32, (8, count), 1) // block) * CAP
    slot = jnp.where(along > 0, rank.astype(jnp.int32) + start, slots)[:1, :]
    place = (lax.broadcasted_iota(jnp.int32, (slots, count), 0) == slot)
    place = place.astype(jnp.float32).astype(jnp.bfloat16)
    chosen = jnp.broadcast_to((down > 0).astype(jnp.float32), (count, LANES))
    rank = jnp.dot(after, chosen.astype(jnp.bfloat16), preferred_element_type=jnp.float32)
    start = (lax.broadcasted_iota(jnp.int32, (count, 1), 0) // block) * CAP
    slot = rank[:, :1].astype(jnp.int32) + start
    combine = jnp.where(
        lax.broadcasted_iota(jnp.int32, (count, slots), 1) == slot, down / denominator, 0.0
    ).astype(jnp.bfloat16)
    return place, combine


def block_copies(block_refs, rows_ref, sems):
    block = block_refs[0].shape[0]
    return [
        pltpu.make_async_copy(ref, rows_ref.at[pl.ds(i * block, block), :], sems.at[i])
        for i, ref in enumerate(block_refs)
    ]


def weight_pieces(gate_hbm, up_hbm, down_hbm, deep, steps):
    cuts = [pl.ds(j * deep, deep) for j in range(steps)]
    pieces = [hbm.at[c, :] for c in cuts for hbm in (gate_hbm, up_hbm)]
    return cuts, pieces + [down_hbm.at[:, c] for c in cuts]


def early_kernel(blocks, expert_ref, *refs):
    block_refs, refs = refs[:blocks], refs[blocks:]
    gate_hbm, up_hbm, items_ref, combine_ref, first_ref = refs[:5]
    rows_ref, sems, weight_sems = refs[5:]
    ahead, deep = first_ref.shape[:2]
    width = items_ref.shape[1]
    steps = width // deep
    copies = block_copies(block_refs, rows_ref, sems)
    pieces = [hbm.at[pl.ds(j * deep, deep), :] for j in range(steps) for hbm in (gate_hbm, up_hbm)]
    near = [
        pltpu.make_async_copy(pieces[i], first_ref.at[i], weight_sems.at[i]) for i in range(ahead)
    ]
    for copy in copies + near:
        copy.start()
    for copy in copies:
        copy.wait()
    place, combine = routing(rows_ref[:, width:], expert_ref[0], block_refs[0].shape[0])
    combine_ref[...] = combine
    for j in range(steps):
        c = pl.ds(j * deep, deep)
        items = jnp.dot(place, rows_ref[:, c], preferred_element_type=jnp.float32)
        items_ref[:, c] = items.astype(jnp.bfloat16)
    for copy in near:
        copy.wait()


def early_part(expert, blocks, w_gate, w_up):
    n = len(blocks)
    block, total = blocks[0].shape
    width, units = total - LANES, w_gate.shape[1]
    slots = n * CAP
    limit = 2 * n * block * total + 4 * slots * width + (6 << 20)
    items, combine, first = pl.pallas_call(
        functools.partial(early_kernel, n),
        out_shape=[
            jax.ShapeDtypeStruct((slots, width), jnp.bfloat16),
            jax.ShapeDtypeStruct((n * block, slots), jnp.bfloat16),
            pltpu.VMEM((EARLY, units, units), jnp.bfloat16),
        ],
        in_specs=[SMEM] + [ANY] * n + [HBM, HBM],
        out_specs=[VMEM] * 3,
        scratch_shapes=[
            pltpu.VMEM((n * block, total), jnp.bfloat16),
            pltpu.SemaphoreType.DMA((n,)),
            pltpu.SemaphoreType.DMA((EARLY,)),
        ],
        compiler_params=pltpu.CompilerParams(vmem_limit_bytes=limit),
        cost_estimate=pl.CostEstimate(
            flops=2 * slots * n * block * width,
            bytes_accessed=EARLY * units * units * 2,
            transcendentals=0,
        ),
        name="early",
    )(expert, *blocks, w_gate, w_up)
    return items, combine, pltpu.with_memory_space_constraint(first, pltpu.VMEM)


def expert_kernel(blocks, expert_ref, *refs):
    block_refs, refs = refs[:blocks], refs[blocks:]
    items_ref, combine_ref, first_ref, gate_hbm, up_hbm, down_hbm = refs[:6]
    outs, refs = refs[6:-7], refs[-7:]
    rows_ref, hidden_ref, ring_ref, gate_sum, up_sum, sems, weight_sems = refs
    ahead = first_ref.shape[0]
    block, width = outs[0].shape
    slots, deep = hidden_ref.shape
    steps = width // deep
    ready = items_ref.shape[0]
    copies = block_copies(block_refs, rows_ref, sems)
    cuts, pieces = weight_pieces(gate_hbm, up_hbm, down_hbm, deep, steps)
    near = [
        pltpu.make_async_copy(piece, ring_ref.at[i % RING], weight_sems.at[i % RING])
        for i, piece in enumerate(pieces[ahead:])
    ]
    for copy in copies + near[: RING - 1]:
        copy.start()
    for copy in copies:
        copy.wait()
    place, combine = routing(rows_ref[:, width:], expert_ref[0], block)

    def weights(i):
        if i < ahead:
            return first_ref[i]
        i -= ahead
        near[i].wait()
        if i + RING - 1 < len(near):
            near[i + RING - 1].start()
        return ring_ref[i % RING]

    for j, c in enumerate(cuts):
        items = jnp.dot(place, rows_ref[:, c], preferred_element_type=jnp.float32)
        items = jnp.concatenate([items_ref[:, c], items.astype(jnp.bfloat16)], axis=0)
        gate = jnp.dot(items, weights(2 * j), preferred_element_type=jnp.float32)
        up = jnp.dot(items, weights(2 * j + 1), preferred_element_type=jnp.float32)
        if j > 0:
            gate, up = gate_sum[...] + gate, up_sum[...] + up
        gate_sum[...], up_sum[...] = gate, up
    gate = gate_sum[...]
    hidden_ref[...] = (gate / (1.0 + jnp.exp(-gate)) * up_sum[...]).astype(jnp.bfloat16)

    for j, c in enumerate(cuts):
        piece = jnp.dot(hidden_ref[...], weights(2 * steps + j), preferred_element_type=jnp.float32)
        piece = piece.astype(jnp.bfloat16)
        part = jnp.dot(combine_ref[...], piece[:ready], preferred_element_type=jnp.float32)
        rest = jnp.dot(combine, piece[ready:], preferred_element_type=jnp.float32)
        part, rest = part.astype(jnp.bfloat16), rest.astype(jnp.bfloat16)
        for i, out in enumerate(outs):
            k = i * block
            out[:, c] = part[k : k + block] if k < part.shape[0] else rest[k - part.shape[0] :][:block]


def expert_part(expert, blocks, early, w_gate, w_up, w_down):
    n = len(blocks)
    block, total = blocks[0].shape
    width, units = total - LANES, w_gate.shape[1]
    slots = early[0].shape[0] + n * CAP
    outs = early[1].shape[0] // block + n
    flops = 2 * slots * units * width * 3
    weights = [pltpu.with_memory_space_constraint(w, pltpu.HBM) for w in (w_gate, w_up, w_down)]
    limit = 2 * RING * units * units + 8 * slots * units + 2 * outs * block * width + (8 << 20)
    return pl.pallas_call(
        functools.partial(expert_kernel, n),
        out_shape=[jax.ShapeDtypeStruct((block, width), jnp.bfloat16)] * outs,
        in_specs=[SMEM] + [ANY] * n + [VMEM] * 3 + [HBM] * 3,
        out_specs=[VMEM] * outs,
        scratch_shapes=[
            pltpu.VMEM((n * block, total), jnp.bfloat16),
            pltpu.VMEM((slots, units), jnp.bfloat16),
            pltpu.VMEM((RING, units, units), jnp.bfloat16),
            pltpu.VMEM((slots, units), jnp.float32),
            pltpu.VMEM((slots, units), jnp.float32),
            pltpu.SemaphoreType.DMA((n,)),
            pltpu.SemaphoreType.DMA((RING,)),
        ],
        compiler_params=pltpu.CompilerParams(vmem_limit_bytes=limit),
        cost_estimate=pl.CostEstimate(
            flops=flops, bytes_accessed=w_down.size * 6, transcendentals=0
        ),
        name="expert",
    )(expert, *blocks, *early, *weights)


def add_kernel(count, *refs):
    total = refs[0][...].astype(jnp.float32)
    for term in refs[1:count]:
        total = total + term[...].astype(jnp.float32)
    refs[-1][...] = total.astype(refs[-1].dtype)


def add(terms, after=()):
    return pl.pallas_call(
        functools.partial(add_kernel, len(terms)),
        out_shape=jax.ShapeDtypeStruct(terms[0].shape, jnp.bfloat16),
        in_specs=[VMEM] * len(terms) + [ANY] * len(after),
        out_specs=VMEM,
        compiler_params=pltpu.CompilerParams(vmem_limit_bytes=4 << 20),
        cost_estimate=pl.CostEstimate(flops=1, bytes_accessed=1, transcendentals=0),
        name="add",
    )(*terms, *after)


def on_device(rows_in, routes, comb_num, w_gate, w_up, w_down):
    n = lax.axis_size("local")
    me = lax.axis_index("local")
    expert = (me // (n // E)).astype(jnp.int32).reshape(1)
    planes = range(n - 4, -1, -4)

    own = pack(rows_in, routes, comb_num)
    got = {0: own}
    for k in planes[:-1]:
        got[k] = exchange(own, k)
    got[2] = exchange(own, 2)
    got[1] = exchange(own, 1)
    first, second = planes[0], planes[1]
    soon = [k | i for k in (first, 0) for i in range(4)]
    late = [k | i for k in planes[1:-1] for i in range(4)]
    got[first | 2] = exchange(got[first], 2)
    for k in soon:
        if k % 2:
            got[k] = exchange(got[k - 1], 1)
    weights = [pltpu.with_memory_space_constraint(w, pltpu.HBM) for w in (w_gate, w_up)]
    items, *early = early_part(expert, [got[k] for k in soon], *weights)
    source, items = lax.optimization_barrier((got[second], items))
    for k in planes[1:-1]:
        got[k | 2] = exchange(source if k == second else got[k], 2)
    for k in late:
        if k % 2:
            got[k] = exchange(got[k - 1], 1)
    outs = expert_part(expert, [got[k] for k in late], (items, *early), w_gate, w_up, w_down)
    parts = dict(zip(soon + late, outs))

    def pair(k, after=()):
        return exchange(add([parts[k | 2], exchange(parts[k | 3], 1)], after), 2)

    def home(k, come, after):
        return add([parts[k], exchange(parts[k | 1], 1), come], after)

    turns = [first, 4, *planes[1:-2]]
    come = {k: pair(k) for k in turns}
    halves = {k: home(k, come[k], ()) for k in turns}
    came = {k: exchange(halves[k], k) for k in turns}
    come[0] = pair(0, (came[first], *halves.values()))
    return add([home(0, come[0], ()), *came.values()])


def solution(mesh):
    in_specs = (
        P(("parts", "local"), None),
        P(("parts", "local"), None),
        P(("parts", "local"), None),
        P(None, "local"),
        P(None, "local"),
        P("local", None),
    )
    out_specs = P(("parts", "local"), None)
    return jax.shard_map(
        on_device, mesh=mesh, in_specs=in_specs, out_specs=out_specs, check_vma=False
    )
```

```python
import functools

import jax
import jax.numpy as jnp
from jax import lax
from jax.experimental import pallas as pl
from jax.experimental.pallas import tpu as pltpu
from jax.sharding import PartitionSpec as P

E = 16
CAP = 8
LANES = 128
RING = 7
EARLY = 6
denominator = 64.0
VMEM = pl.BlockSpec(memory_space=pltpu.VMEM)
SMEM = pl.BlockSpec(memory_space=pltpu.SMEM)
ANY = pl.BlockSpec(memory_space=pl.ANY)
HBM = pl.BlockSpec(memory_space=pltpu.HBM)


def exchange(x, distance):
    n = lax.axis_size("local")
    return lax.ppermute(x, "local", [(i, i ^ distance) for i in range(n)])


def pack_kernel(rows_ref, routes_ref, comb_ref, out_ref):
    rows, width = rows_ref.shape
    out_ref[:, :width] = rows_ref[...]
    sub = lax.broadcasted_iota(jnp.int32, (LANES, rows), 0)
    table = jnp.zeros((LANES, rows), jnp.int32)
    for k in range(routes_ref.shape[0]):
        table = jnp.where(sub == routes_ref[k : k + 1, :], comb_ref[k : k + 1, :], table)
    same = lax.broadcasted_iota(jnp.int32, (rows, rows), 0) == lax.broadcasted_iota(jnp.int32, (rows, rows), 1)
    turned = lax.dot_general(
        same.astype(jnp.float32).astype(jnp.bfloat16),
        table.astype(jnp.float32).astype(jnp.bfloat16),
        (((1,), (1,)), ((), ())), preferred_element_type=jnp.float32,
    )
    out_ref[:, width:] = turned.astype(jnp.bfloat16)


def pack(rows, routes, comb):
    return pl.pallas_call(
        pack_kernel,
        out_shape=jax.ShapeDtypeStruct((rows.shape[0], rows.shape[1] + LANES), rows.dtype),
        in_specs=[VMEM] * 3,
        out_specs=VMEM,
        name="pack",
    )(rows, routes.T, comb.T)


def routing(table, expert, block):
    count = table.shape[0]
    slots = count // block * CAP
    mine = (lax.broadcasted_iota(jnp.int32, (8, LANES), 1) == expert).astype(jnp.float32)
    along = lax.dot_general(
        mine.astype(jnp.bfloat16), table, (((1,), (1,)), ((), ())),
        preferred_element_type=jnp.float32,
    )
    down = jnp.sum(table.astype(jnp.float32) * mine[:1, :], axis=1, keepdims=True)
    r = lax.broadcasted_iota(jnp.int32, (count, count), 0)
    s = lax.broadcasted_iota(jnp.int32, (count, count), 1)
    same = (r // block) == (s // block)
    before = (same & (r < s)).astype(jnp.float32).astype(jnp.bfloat16)
    after = (same & (s < r)).astype(jnp.float32).astype(jnp.bfloat16)
    chosen = (along > 0).astype(jnp.float32)
    rank = jnp.dot(chosen.astype(jnp.bfloat16), before, preferred_element_type=jnp.float32)
    start = (lax.broadcasted_iota(jnp.int32, (8, count), 1) // block) * CAP
    slot = jnp.where(along > 0, rank.astype(jnp.int32) + start, slots)[:1, :]
    place = (lax.broadcasted_iota(jnp.int32, (slots, count), 0) == slot)
    place = place.astype(jnp.float32).astype(jnp.bfloat16)
    chosen = jnp.broadcast_to((down > 0).astype(jnp.float32), (count, LANES))
    rank = jnp.dot(after, chosen.astype(jnp.bfloat16), preferred_element_type=jnp.float32)
    start = (lax.broadcasted_iota(jnp.int32, (count, 1), 0) // block) * CAP
    slot = rank[:, :1].astype(jnp.int32) + start
    combine = jnp.where(
        lax.broadcasted_iota(jnp.int32, (count, slots), 1) == slot, down / denominator, 0.0
    ).astype(jnp.bfloat16)
    return place, combine


def block_copies(block_refs, rows_ref, sems):
    block = block_refs[0].shape[0]
    return [
        pltpu.make_async_copy(ref, rows_ref.at[pl.ds(i * block, block), :], sems.at[i])
        for i, ref in enumerate(block_refs)
    ]


def weight_pieces(gate_hbm, up_hbm, down_hbm, deep, steps):
    cuts = [pl.ds(j * deep, deep) for j in range(steps)]
    pieces = [hbm.at[c, :] for c in cuts for hbm in (gate_hbm, up_hbm)]
    return cuts, pieces + [down_hbm.at[:, c] for c in cuts]


def early_kernel(blocks, expert_ref, *refs):
    block_refs, refs = refs[:blocks], refs[blocks:]
    gate_hbm, up_hbm, items_ref, combine_ref, first_ref = refs[:5]
    rows_ref, sems, weight_sems = refs[5:]
    ahead, deep = first_ref.shape[:2]
    width = items_ref.shape[1]
    steps = width // deep
    copies = block_copies(block_refs, rows_ref, sems)
    pieces = [hbm.at[pl.ds(j * deep, deep), :] for j in range(steps) for hbm in (gate_hbm, up_hbm)]
    near = [
        pltpu.make_async_copy(pieces[i], first_ref.at[i], weight_sems.at[i]) for i in range(ahead)
    ]
    for copy in copies + near:
        copy.start()
    for copy in copies:
        copy.wait()
    place, combine = routing(rows_ref[:, width:], expert_ref[0], block_refs[0].shape[0])
    combine_ref[...] = combine
    for j in range(steps):
        c = pl.ds(j * deep, deep)
        items = jnp.dot(place, rows_ref[:, c], preferred_element_type=jnp.float32)
        items_ref[:, c] = items.astype(jnp.bfloat16)
    for copy in near:
        copy.wait()


def early_part(expert, blocks, w_gate, w_up):
    n = len(blocks)
    block, total = blocks[0].shape
    width, units = total - LANES, w_gate.shape[1]
    slots = n * CAP
    limit = 2 * n * block * total + 4 * slots * width + (6 << 20)
    items, combine, first = pl.pallas_call(
        functools.partial(early_kernel, n),
        out_shape=[
            jax.ShapeDtypeStruct((slots, width), jnp.bfloat16),
            jax.ShapeDtypeStruct((n * block, slots), jnp.bfloat16),
            pltpu.VMEM((EARLY, units, units), jnp.bfloat16),
        ],
        in_specs=[SMEM] + [ANY] * n + [HBM, HBM],
        out_specs=[VMEM] * 3,
        scratch_shapes=[
            pltpu.VMEM((n * block, total), jnp.bfloat16),
            pltpu.SemaphoreType.DMA((n,)),
            pltpu.SemaphoreType.DMA((EARLY,)),
        ],
        compiler_params=pltpu.CompilerParams(vmem_limit_bytes=limit),
        cost_estimate=pl.CostEstimate(
            flops=2 * slots * n * block * width,
            bytes_accessed=EARLY * units * units * 2,
            transcendentals=0,
        ),
        name="early",
    )(expert, *blocks, w_gate, w_up)
    return items, combine, pltpu.with_memory_space_constraint(first, pltpu.VMEM)


def expert_kernel(blocks, expert_ref, *refs):
    block_refs, refs = refs[:blocks], refs[blocks:]
    items_ref, combine_ref, first_ref, gate_hbm, up_hbm, down_hbm = refs[:6]
    outs, refs = refs[6:-7], refs[-7:]
    rows_ref, hidden_ref, ring_ref, gate_sum, up_sum, sems, weight_sems = refs
    ahead = first_ref.shape[0]
    block, width = outs[0].shape
    slots, deep = hidden_ref.shape
    steps = width // deep
    ready = items_ref.shape[0]
    copies = block_copies(block_refs, rows_ref, sems)
    cuts, pieces = weight_pieces(gate_hbm, up_hbm, down_hbm, deep, steps)
    near = [
        pltpu.make_async_copy(piece, ring_ref.at[i % RING], weight_sems.at[i % RING])
        for i, piece in enumerate(pieces[ahead:])
    ]
    for copy in copies + near[: RING - 1]:
        copy.start()
    for copy in copies:
        copy.wait()
    place, combine = routing(rows_ref[:, width:], expert_ref[0], block)

    def weights(i):
        if i < ahead:
            return first_ref[i]
        i -= ahead
        near[i].wait()
        if i + RING - 1 < len(near):
            near[i + RING - 1].start()
        return ring_ref[i % RING]

    for j, c in enumerate(cuts):
        items = jnp.dot(place, rows_ref[:, c], preferred_element_type=jnp.float32)
        items = jnp.concatenate([items_ref[:, c], items.astype(jnp.bfloat16)], axis=0)
        gate = jnp.dot(items, weights(2 * j), preferred_element_type=jnp.float32)
        up = jnp.dot(items, weights(2 * j + 1), preferred_element_type=jnp.float32)
        if j > 0:
            gate, up = gate_sum[...] + gate, up_sum[...] + up
        gate_sum[...], up_sum[...] = gate, up
    gate = gate_sum[...]
    hidden_ref[...] = (gate / (1.0 + jnp.exp(-gate)) * up_sum[...]).astype(jnp.bfloat16)

    for j, c in enumerate(cuts):
        piece = jnp.dot(hidden_ref[...], weights(2 * steps + j), preferred_element_type=jnp.float32)
        piece = piece.astype(jnp.bfloat16)
        part = jnp.dot(combine_ref[...], piece[:ready], preferred_element_type=jnp.float32)
        rest = jnp.dot(combine, piece[ready:], preferred_element_type=jnp.float32)
        part, rest = part.astype(jnp.bfloat16), rest.astype(jnp.bfloat16)
        for i, out in enumerate(outs):
            k = i * block
            out[:, c] = part[k : k + block] if k < part.shape[0] else rest[k - part.shape[0] :][:block]


def expert_part(expert, blocks, early, w_gate, w_up, w_down):
    n = len(blocks)
    block, total = blocks[0].shape
    width, units = total - LANES, w_gate.shape[1]
    slots = early[0].shape[0] + n * CAP
    outs = early[1].shape[0] // block + n
    flops = 2 * slots * units * width * 3
    weights = [pltpu.with_memory_space_constraint(w, pltpu.HBM) for w in (w_gate, w_up, w_down)]
    limit = 2 * RING * units * units + 8 * slots * units + 2 * outs * block * width + (8 << 20)
    return pl.pallas_call(
        functools.partial(expert_kernel, n),
        out_shape=[jax.ShapeDtypeStruct((block, width), jnp.bfloat16)] * outs,
        in_specs=[SMEM] + [ANY] * n + [VMEM] * 3 + [HBM] * 3,
        out_specs=[VMEM] * outs,
        scratch_shapes=[
            pltpu.VMEM((n * block, total), jnp.bfloat16),
            pltpu.VMEM((slots, units), jnp.bfloat16),
            pltpu.VMEM((RING, units, units), jnp.bfloat16),
            pltpu.VMEM((slots, units), jnp.float32),
            pltpu.VMEM((slots, units), jnp.float32),
            pltpu.SemaphoreType.DMA((n,)),
            pltpu.SemaphoreType.DMA((RING,)),
        ],
        compiler_params=pltpu.CompilerParams(vmem_limit_bytes=limit),
        cost_estimate=pl.CostEstimate(
            flops=flops, bytes_accessed=w_down.size * 6, transcendentals=0
        ),
        name="expert",
    )(expert, *blocks, *early, *weights)


def add_kernel(count, *refs):
    total = refs[0][...].astype(jnp.float32)
    for term in refs[1:count]:
        total = total + term[...].astype(jnp.float32)
    refs[-1][...] = total.astype(refs[-1].dtype)


def add(terms, after=()):
    return pl.pallas_call(
        functools.partial(add_kernel, len(terms)),
        out_shape=jax.ShapeDtypeStruct(terms[0].shape, jnp.bfloat16),
        in_specs=[VMEM] * len(terms) + [ANY] * len(after),
        out_specs=VMEM,
        compiler_params=pltpu.CompilerParams(vmem_limit_bytes=4 << 20),
        cost_estimate=pl.CostEstimate(flops=1, bytes_accessed=1, transcendentals=0),
        name="add",
    )(*terms, *after)


def on_device(rows_in, routes, comb_num, w_gate, w_up, w_down):
    n = lax.axis_size("local")
    me = lax.axis_index("local")
    expert = (me // (n // E)).astype(jnp.int32).reshape(1)
    planes = range(n - 4, -1, -4)

    own = pack(rows_in, routes, comb_num)
    got = {0: own}
    for k in planes[:-1]:
        got[k] = exchange(own, k)
    got[2] = exchange(own, 2)
    got[1] = exchange(own, 1)
    first, second = planes[0], planes[1]
    soon = [k | i for k in (first, 0) for i in range(4)]
    late = [k | i for k in planes[1:-1] for i in range(4)]
    got[first | 2] = exchange(got[first], 2)
    for k in soon:
        if k % 2:
            got[k] = exchange(got[k - 1], 1)
    weights = [pltpu.with_memory_space_constraint(w, pltpu.HBM) for w in (w_gate, w_up)]
    items, *early = early_part(expert, [got[k] for k in soon], *weights)
    source, items = lax.optimization_barrier((got[second], items))
    for k in planes[1:-1]:
        got[k | 2] = exchange(source if k == second else got[k], 2)
    for k in late:
        if k % 2:
            got[k] = exchange(got[k - 1], 1)
    outs = expert_part(expert, [got[k] for k in late], (items, *early), w_gate, w_up, w_down)
    parts = dict(zip(soon + late, outs))

    def pair(k, after=()):
        return exchange(add([parts[k | 2], exchange(parts[k | 3], 1)], after), 2)

    def home(k, come, after):
        return add([parts[k], exchange(parts[k | 1], 1), come], after)

    turns = [first, 4, *planes[1:-2]]
    come = {k: pair(k) for k in turns}
    halves = {k: home(k, come[k], ()) for k in turns}
    came = {k: exchange(halves[k], k) for k in turns}
    come[0] = pair(0, (came[first],))
    return add([home(0, come[0], ()), *came.values()])


def solution(mesh):
    in_specs = (
        P(("parts", "local"), None),
        P(("parts", "local"), None),
        P(("parts", "local"), None),
        P(None, "local"),
        P(None, "local"),
        P("local", None),
    )
    out_specs = P(("parts", "local"), None)
    return jax.shard_map(
        on_device, mesh=mesh, in_specs=in_specs, out_specs=out_specs, check_vma=False
    )
```

```python
import functools

import jax
import jax.numpy as jnp
from jax import lax
from jax.experimental import pallas as pl
from jax.experimental.pallas import tpu as pltpu
from jax.sharding import PartitionSpec as P

E = 16
CAP = 8
LANES = 128
RING = 7
EARLY = 8
denominator = 64.0
VMEM = pl.BlockSpec(memory_space=pltpu.VMEM)
SMEM = pl.BlockSpec(memory_space=pltpu.SMEM)
ANY = pl.BlockSpec(memory_space=pl.ANY)
HBM = pl.BlockSpec(memory_space=pltpu.HBM)


def exchange(x, distance):
    n = lax.axis_size("local")
    return lax.ppermute(x, "local", [(i, i ^ distance) for i in range(n)])


def pack_kernel(rows_ref, routes_ref, comb_ref, out_ref):
    rows, width = rows_ref.shape
    out_ref[:, :width] = rows_ref[...]
    sub = lax.broadcasted_iota(jnp.int32, (LANES, rows), 0)
    table = jnp.zeros((LANES, rows), jnp.int32)
    for k in range(routes_ref.shape[0]):
        table = jnp.where(sub == routes_ref[k : k + 1, :], comb_ref[k : k + 1, :], table)
    same = lax.broadcasted_iota(jnp.int32, (rows, rows), 0) == lax.broadcasted_iota(jnp.int32, (rows, rows), 1)
    turned = lax.dot_general(
        same.astype(jnp.float32).astype(jnp.bfloat16),
        table.astype(jnp.float32).astype(jnp.bfloat16),
        (((1,), (1,)), ((), ())), preferred_element_type=jnp.float32,
    )
    out_ref[:, width:] = turned.astype(jnp.bfloat16)


def pack(rows, routes, comb):
    return pl.pallas_call(
        pack_kernel,
        out_shape=jax.ShapeDtypeStruct((rows.shape[0], rows.shape[1] + LANES), rows.dtype),
        in_specs=[VMEM] * 3,
        out_specs=VMEM,
        name="pack",
    )(rows, routes.T, comb.T)


def routing(table, expert, block):
    count = table.shape[0]
    slots = count // block * CAP
    mine = (lax.broadcasted_iota(jnp.int32, (8, LANES), 1) == expert).astype(jnp.float32)
    along = lax.dot_general(
        mine.astype(jnp.bfloat16), table, (((1,), (1,)), ((), ())),
        preferred_element_type=jnp.float32,
    )
    down = jnp.sum(table.astype(jnp.float32) * mine[:1, :], axis=1, keepdims=True)
    r = lax.broadcasted_iota(jnp.int32, (count, count), 0)
    s = lax.broadcasted_iota(jnp.int32, (count, count), 1)
    same = (r // block) == (s // block)
    before = (same & (r < s)).astype(jnp.float32).astype(jnp.bfloat16)
    after = (same & (s < r)).astype(jnp.float32).astype(jnp.bfloat16)
    chosen = (along > 0).astype(jnp.float32)
    rank = jnp.dot(chosen.astype(jnp.bfloat16), before, preferred_element_type=jnp.float32)
    start = (lax.broadcasted_iota(jnp.int32, (8, count), 1) // block) * CAP
    slot = jnp.where(along > 0, rank.astype(jnp.int32) + start, slots)[:1, :]
    place = (lax.broadcasted_iota(jnp.int32, (slots, count), 0) == slot)
    place = place.astype(jnp.float32).astype(jnp.bfloat16)
    chosen = jnp.broadcast_to((down > 0).astype(jnp.float32), (count, LANES))
    rank = jnp.dot(after, chosen.astype(jnp.bfloat16), preferred_element_type=jnp.float32)
    start = (lax.broadcasted_iota(jnp.int32, (count, 1), 0) // block) * CAP
    slot = rank[:, :1].astype(jnp.int32) + start
    combine = jnp.where(
        lax.broadcasted_iota(jnp.int32, (count, slots), 1) == slot, down / denominator, 0.0
    ).astype(jnp.bfloat16)
    return place, combine


def block_copies(block_refs, rows_ref, sems):
    block = block_refs[0].shape[0]
    return [
        pltpu.make_async_copy(ref, rows_ref.at[pl.ds(i * block, block), :], sems.at[i])
        for i, ref in enumerate(block_refs)
    ]


def weight_pieces(gate_hbm, up_hbm, down_hbm, deep, steps):
    cuts = [pl.ds(j * deep, deep) for j in range(steps)]
    pieces = [hbm.at[c, :] for c in cuts for hbm in (gate_hbm, up_hbm)]
    return cuts, pieces + [down_hbm.at[:, c] for c in cuts]


def early_kernel(blocks, expert_ref, *refs):
    block_refs, refs = refs[:blocks], refs[blocks:]
    gate_hbm, up_hbm, items_ref, combine_ref, first_ref = refs[:5]
    rows_ref, sems, weight_sems = refs[5:]
    ahead, deep = first_ref.shape[:2]
    width = items_ref.shape[1]
    steps = width // deep
    copies = block_copies(block_refs, rows_ref, sems)
    pieces = [hbm.at[pl.ds(j * deep, deep), :] for j in range(steps) for hbm in (gate_hbm, up_hbm)]
    near = [
        pltpu.make_async_copy(pieces[i], first_ref.at[i], weight_sems.at[i]) for i in range(ahead)
    ]
    for copy in copies + near:
        copy.start()
    for copy in copies:
        copy.wait()
    place, combine = routing(rows_ref[:, width:], expert_ref[0], block_refs[0].shape[0])
    combine_ref[...] = combine
    for j in range(steps):
        c = pl.ds(j * deep, deep)
        items = jnp.dot(place, rows_ref[:, c], preferred_element_type=jnp.float32)
        items_ref[:, c] = items.astype(jnp.bfloat16)
    for copy in near:
        copy.wait()


def early_part(expert, blocks, w_gate, w_up):
    n = len(blocks)
    block, total = blocks[0].shape
    width, units = total - LANES, w_gate.shape[1]
    slots = n * CAP
    limit = 2 * n * block * total + 4 * slots * width + (6 << 20)
    items, combine, first = pl.pallas_call(
        functools.partial(early_kernel, n),
        out_shape=[
            jax.ShapeDtypeStruct((slots, width), jnp.bfloat16),
            jax.ShapeDtypeStruct((n * block, slots), jnp.bfloat16),
            pltpu.VMEM((EARLY, units, units), jnp.bfloat16),
        ],
        in_specs=[SMEM] + [ANY] * n + [HBM, HBM],
        out_specs=[VMEM] * 3,
        scratch_shapes=[
            pltpu.VMEM((n * block, total), jnp.bfloat16),
            pltpu.SemaphoreType.DMA((n,)),
            pltpu.SemaphoreType.DMA((EARLY,)),
        ],
        compiler_params=pltpu.CompilerParams(vmem_limit_bytes=limit),
        cost_estimate=pl.CostEstimate(
            flops=2 * slots * n * block * width,
            bytes_accessed=EARLY * units * units * 2,
            transcendentals=0,
        ),
        name="early",
    )(expert, *blocks, w_gate, w_up)
    return items, combine, pltpu.with_memory_space_constraint(first, pltpu.VMEM)


def expert_kernel(blocks, expert_ref, *refs):
    block_refs, refs = refs[:blocks], refs[blocks:]
    items_ref, combine_ref, first_ref, gate_hbm, up_hbm, down_hbm = refs[:6]
    outs, refs = refs[6:-7], refs[-7:]
    rows_ref, hidden_ref, ring_ref, gate_sum, up_sum, sems, weight_sems = refs
    ahead = first_ref.shape[0]
    block, width = outs[0].shape
    slots, deep = hidden_ref.shape
    steps = width // deep
    ready = items_ref.shape[0]
    copies = block_copies(block_refs, rows_ref, sems)
    cuts, pieces = weight_pieces(gate_hbm, up_hbm, down_hbm, deep, steps)
    near = [
        pltpu.make_async_copy(piece, ring_ref.at[i % RING], weight_sems.at[i % RING])
        for i, piece in enumerate(pieces[ahead:])
    ]
    for copy in copies + near[: RING - 1]:
        copy.start()
    for copy in copies:
        copy.wait()
    place, combine = routing(rows_ref[:, width:], expert_ref[0], block)

    def weights(i):
        if i < ahead:
            return first_ref[i]
        i -= ahead
        near[i].wait()
        if i + RING - 1 < len(near):
            near[i + RING - 1].start()
        return ring_ref[i % RING]

    for j, c in enumerate(cuts):
        items = jnp.dot(place, rows_ref[:, c], preferred_element_type=jnp.float32)
        items = jnp.concatenate([items_ref[:, c], items.astype(jnp.bfloat16)], axis=0)
        gate = jnp.dot(items, weights(2 * j), preferred_element_type=jnp.float32)
        up = jnp.dot(items, weights(2 * j + 1), preferred_element_type=jnp.float32)
        if j > 0:
            gate, up = gate_sum[...] + gate, up_sum[...] + up
        gate_sum[...], up_sum[...] = gate, up
    gate = gate_sum[...]
    hidden_ref[...] = (gate / (1.0 + jnp.exp(-gate)) * up_sum[...]).astype(jnp.bfloat16)

    for j, c in enumerate(cuts):
        piece = jnp.dot(hidden_ref[...], weights(2 * steps + j), preferred_element_type=jnp.float32)
        piece = piece.astype(jnp.bfloat16)
        part = jnp.dot(combine_ref[...], piece[:ready], preferred_element_type=jnp.float32)
        rest = jnp.dot(combine, piece[ready:], preferred_element_type=jnp.float32)
        part, rest = part.astype(jnp.bfloat16), rest.astype(jnp.bfloat16)
        for i, out in enumerate(outs):
            k = i * block
            out[:, c] = part[k : k + block] if k < part.shape[0] else rest[k - part.shape[0] :][:block]


def expert_part(expert, blocks, early, w_gate, w_up, w_down):
    n = len(blocks)
    block, total = blocks[0].shape
    width, units = total - LANES, w_gate.shape[1]
    slots = early[0].shape[0] + n * CAP
    outs = early[1].shape[0] // block + n
    flops = 2 * slots * units * width * 3
    weights = [pltpu.with_memory_space_constraint(w, pltpu.HBM) for w in (w_gate, w_up, w_down)]
    limit = 2 * RING * units * units + 8 * slots * units + 2 * outs * block * width + (8 << 20)
    return pl.pallas_call(
        functools.partial(expert_kernel, n),
        out_shape=[jax.ShapeDtypeStruct((block, width), jnp.bfloat16)] * outs,
        in_specs=[SMEM] + [ANY] * n + [VMEM] * 3 + [HBM] * 3,
        out_specs=[VMEM] * outs,
        scratch_shapes=[
            pltpu.VMEM((n * block, total), jnp.bfloat16),
            pltpu.VMEM((slots, units), jnp.bfloat16),
            pltpu.VMEM((RING, units, units), jnp.bfloat16),
            pltpu.VMEM((slots, units), jnp.float32),
            pltpu.VMEM((slots, units), jnp.float32),
            pltpu.SemaphoreType.DMA((n,)),
            pltpu.SemaphoreType.DMA((RING,)),
        ],
        compiler_params=pltpu.CompilerParams(vmem_limit_bytes=limit),
        cost_estimate=pl.CostEstimate(
            flops=flops, bytes_accessed=w_down.size * 6, transcendentals=0
        ),
        name="expert",
    )(expert, *blocks, *early, *weights)


def add_kernel(count, *refs):
    total = refs[0][...].astype(jnp.float32)
    for term in refs[1:count]:
        total = total + term[...].astype(jnp.float32)
    refs[-1][...] = total.astype(refs[-1].dtype)


def add(terms, after=()):
    return pl.pallas_call(
        functools.partial(add_kernel, len(terms)),
        out_shape=jax.ShapeDtypeStruct(terms[0].shape, jnp.bfloat16),
        in_specs=[VMEM] * len(terms) + [ANY] * len(after),
        out_specs=VMEM,
        compiler_params=pltpu.CompilerParams(vmem_limit_bytes=4 << 20),
        cost_estimate=pl.CostEstimate(flops=1, bytes_accessed=1, transcendentals=0),
        name="add",
    )(*terms, *after)


def on_device(rows_in, routes, comb_num, w_gate, w_up, w_down):
    n = lax.axis_size("local")
    me = lax.axis_index("local")
    expert = (me // (n // E)).astype(jnp.int32).reshape(1)
    planes = range(n - 4, -1, -4)

    own = pack(rows_in, routes, comb_num)
    got = {0: own}
    for k in planes[:-1]:
        got[k] = exchange(own, k)
    got[2] = exchange(own, 2)
    got[1] = exchange(own, 1)
    first, second = planes[0], planes[1]
    soon = [k | i for k in (first, 0) for i in range(4)]
    late = [k | i for k in planes[1:-1] for i in range(4)]
    got[first | 2] = exchange(got[first], 2)
    for k in soon:
        if k % 2:
            got[k] = exchange(got[k - 1], 1)
    weights = [pltpu.with_memory_space_constraint(w, pltpu.HBM) for w in (w_gate, w_up)]
    items, *early = early_part(expert, [got[k] for k in soon], *weights)
    source, items = lax.optimization_barrier((got[second], items))
    for k in planes[1:-1]:
        got[k | 2] = exchange(source if k == second else got[k], 2)
    for k in late:
        if k % 2:
            got[k] = exchange(got[k - 1], 1)
    outs = expert_part(expert, [got[k] for k in late], (items, *early), w_gate, w_up, w_down)
    parts = dict(zip(soon + late, outs))

    def pair(k, after=()):
        return exchange(add([parts[k | 2], exchange(parts[k | 3], 1)], after), 2)

    def home(k, come, after):
        return add([parts[k], exchange(parts[k | 1], 1), come], after)

    turns = [first, 4, *planes[1:-2]]
    come = {k: pair(k) for k in turns}
    halves = {k: home(k, come[k], ()) for k in turns}
    came = {k: exchange(halves[k], k) for k in turns}
    come[0] = pair(0, (came[first],))
    return add([home(0, come[0], ()), *came.values()])


def solution(mesh):
    in_specs = (
        P(("parts", "local"), None),
        P(("parts", "local"), None),
        P(("parts", "local"), None),
        P(None, "local"),
        P(None, "local"),
        P("local", None),
    )
    out_specs = P(("parts", "local"), None)
    return jax.shard_map(
        on_device, mesh=mesh, in_specs=in_specs, out_specs=out_specs, check_vma=False
    )
```
